128 devices in a mesh: wide: 32 (over z, x, core), narrow: 4 (over y).
Axes of the slice: x: 4, y: 4, z: 4, core: 2. Of those that a mesh axis runs over, the one named last changes fastest.
Arguments:
- flow_field: bfloat16 [256, 64, 16, 512], P('wide', 'narrow'), may hold values from -48 to 48
- fluid_mask: int32 [256, 64, 16], P('wide', 'narrow'), may hold values 0 or 1
- conv_weight: float32 [27, 512], replicated, may hold values from -1 to 1
- latents: bfloat16 [1024, 512], replicated, may hold values from -6 to 6
- w_query1: bfloat16 [512, 512], replicated, may hold values from -0.25 to 0.25
- w_key1: bfloat16 [512, 512], replicated, may hold values from -0.25 to 0.25
- w_value1: bfloat16 [512, 512], replicated, may hold values from -0.25 to 0.25
- w_out1: bfloat16 [512, 512], replicated, may hold values from -0.25 to 0.25
- w_query2: bfloat16 [512, 512], replicated, may hold values from -0.25 to 0.25
- w_key2: bfloat16 [512, 512], replicated, may hold values from -0.25 to 0.25
- w_value2: bfloat16 [512, 512], replicated, may hold values from -0.25 to 0.25
- w_out2: bfloat16 [512, 512], replicated, may hold values from -0.25 to 0.25
Outputs:
- updated_field: float32 [256, 64, 16, 512], P('wide', 'narrow')
The draws below stay inside these ranges and needn't reach their ends.
All inputs are finite; a program needn't handle non-finite values. No bound on the sum of `fluid_mask` on one device may be relied on, other than what follows from the above.
Results may differ from the reference program's by a relative error of at most 0.035.
The reference program's roundings to bfloat16 on the way count: a program that leaves them out, or rounds other values in their place, can miss the bound.
Values may be sent and summed in bfloat16 or wider, within the bound.
A program may use at most 192 MiB of HBM per device.

```python
import math
import jax
import jax.numpy as jnp
from jax import lax

D = 512
HEADS = 8
HEAD_DIM = 64
LATENTS = 1024
NX = 256
NY = 64
NZ = 16


def draw_flow_field(key, part):
    base_key = jax.random.fold_in(jax.random.fold_in(key, 11), 0)
    grid_shape = (NX, NY, NZ, D)
    values = jnp.clip(jax.random.normal(base_key, grid_shape, jnp.float32), -6.0, 6.0)
    return values.astype(jnp.bfloat16)


def draw_latents(key, part):
    entry_key = jax.random.fold_in(jax.random.fold_in(key, 23), 0)
    latent_shape = (LATENTS, D)
    values = jnp.clip(jax.random.normal(entry_key, latent_shape, jnp.float32), -6.0, 6.0)
    return values.astype(jnp.bfloat16)


def set_ends(values, stream_key, smallest, high):
    longest = values.shape.index(max(values.shape))
    spots = []
    for shift in (0, 1):
        where = [jax.random.randint(jax.random.fold_in(stream_key, axis), (), 0, length) for axis, length in enumerate(values.shape)]
        where[longest] = (where[longest] + shift) % values.shape[longest]
        spots.append(tuple(where))
    return values.at[spots[0]].set(smallest).at[spots[1]].set(high)


def centred(rng, extent, spread, limit, dtype=jnp.bfloat16):
    return jnp.clip(spread * jax.random.normal(rng, extent, jnp.float32), -limit, limit).astype(dtype)


def setup_inputs(seed: int = 0) -> dict:
    keys = jax.random.split(jax.random.key(seed), 13)
    flow_field = draw_flow_field(jax.random.fold_in(keys[12], 71), 0)
    fluid_mask = set_ends((jax.random.randint(keys[1], (NX, NY, NZ), 0, 8) < 7).astype(jnp.int32), jax.random.fold_in(keys[1], 1), 0, 1)
    conv_weight = centred(keys[2], (27, D), 0.2, 1.0, jnp.float32)
    latents = draw_latents(jax.random.fold_in(keys[12], 71), 0)
    w_query1 = centred(keys[4], (D, D), D ** -0.5, 0.25)
    w_key1 = centred(keys[5], (D, D), D ** -0.5, 0.25)
    w_value1 = centred(keys[6], (D, D), D ** -0.5, 0.25)
    w_out1 = centred(keys[7], (D, D), D ** -0.5, 0.25)
    w_query2 = centred(keys[8], (D, D), D ** -0.5, 0.25)
    w_key2 = centred(keys[9], (D, D), D ** -0.5, 0.25)
    w_value2 = centred(keys[10], (D, D), D ** -0.5, 0.25)
    w_out2 = centred(keys[11], (D, D), D ** -0.5, 0.25)
    return {"flow_field": flow_field, "fluid_mask": fluid_mask, "conv_weight": conv_weight, "latents": latents, "w_query1": w_query1, "w_key1": w_key1, "w_value1": w_value1, "w_out1": w_out1, "w_query2": w_query2, "w_key2": w_key2, "w_value2": w_value2, "w_out2": w_out2}


def project(row_block, weight):
    return jnp.dot(row_block, weight, preferred_element_type=jnp.float32).astype(jnp.bfloat16)

def heads_first(matrix):
    return matrix.reshape(matrix.shape[0], HEADS, HEAD_DIM).transpose(1, 0, 2)

def score_block(head_queries, head_keys):
    factor = 1.8 / math.sqrt(HEAD_DIM)
    return factor * lax.dot_general(head_queries, head_keys, (((1,), (1,)), ((), ())), preferred_element_type=jnp.float32)

def attend_exact(operands):
    head_queries, head_keys, head_values = operands
    scores = score_block(head_queries, head_keys)
    top_score = lax.optimization_barrier(jnp.max(scores, axis=1, keepdims=True))
    weights = jnp.exp(scores - top_score)
    totals = lax.optimization_barrier(jnp.sum(weights, axis=1, keepdims=True))
    summed = jnp.dot(weights, head_values.astype(jnp.float32), precision=lax.Precision.HIGHEST, preferred_element_type=jnp.float32)
    return summed / totals

def attend_rounded(operands):
    head_queries, head_keys, head_values = operands
    scores = score_block(head_queries, head_keys)
    top_score = lax.optimization_barrier(jnp.max(scores, axis=1, keepdims=True))
    weights = jnp.exp(scores - top_score)
    totals = lax.optimization_barrier(jnp.sum(weights, axis=1, keepdims=True))
    summed = jnp.dot(weights.astype(jnp.bfloat16), head_values, preferred_element_type=jnp.float32)
    return summed / totals

def heads_last(stacked):
    return stacked.transpose(1, 0, 2).reshape(stacked.shape[1], D).astype(jnp.bfloat16)

def reference(flow_field, fluid_mask, conv_weight, latents, w_query1, w_key1, w_value1, w_out1, w_query2, w_key2, w_value2, w_out2):
    masked = flow_field * fluid_mask[:, :, :, None].astype(jnp.bfloat16)
    padded = jnp.pad(masked, ((1, 1), (1, 1), (1, 1), (0, 0)))
    stencil = masked.astype(jnp.float32)
    for offset_x in range(3):
        for offset_y in range(3):
            for offset_z in range(3):
                window = padded[offset_x:offset_x + NX, offset_y:offset_y + NY, offset_z:offset_z + NZ]
                stencil = stencil + window.astype(jnp.float32) * conv_weight[9 * offset_x + 3 * offset_y + offset_z]
    mixed_cells = stencil.astype(jnp.bfloat16).reshape(NX * NY * NZ, D)
    keys1 = project(mixed_cells, w_key1)
    values1 = project(mixed_cells, w_value1)
    queries1 = project(latents, w_query1)
    read1 = heads_last(lax.map(attend_exact, (heads_first(queries1), heads_first(keys1), heads_first(values1))))
    latent_state = (latents.astype(jnp.float32) + jnp.dot(read1, w_out1, preferred_element_type=jnp.float32)).astype(jnp.bfloat16)
    keys2 = project(latent_state, w_key2)
    values2 = project(latent_state, w_value2)
    queries2 = project(mixed_cells, w_query2)
    read2 = heads_last(lax.map(attend_rounded, (heads_first(queries2), heads_first(keys2), heads_first(values2))))
    flat_masked = masked.reshape(NX * NY * NZ, D)
    result = flat_masked.astype(jnp.float32) + jnp.dot(read2, w_out2, preferred_element_type=jnp.float32)
    return result.reshape(NX, NY, NZ, D)
```

```python
import functools
import math

import jax
import jax.numpy as jnp
from jax import lax
from jax.experimental import pallas as pl
from jax.experimental.pallas import tpu as pltpu
from jax.sharding import PartitionSpec as P

HEADS = 8
MESH = pl.DeviceIdType.MESH
F32 = jnp.float32
BF16 = jnp.bfloat16


def dot(a, b):
    return jnp.dot(a, b, preferred_element_type=F32)


def dot_t(a, b):
    return lax.dot_general(a, b, (((1,), (1,)), ((), ())), preferred_element_type=F32)


def vmem():
    return pl.BlockSpec(memory_space=pltpu.VMEM)


def stencil_kernel(
    cells, conv, latents, w_q1, w_k1, w_v1, w_q2,
    q1, k1, v1, q2,
    x_side, y_side, corner, pad, mixed, send_sem, recv_sem,
):
    size_x, size_y, size_z, width = cells.shape
    wide, narrow = lax.axis_index("wide"), lax.axis_index("narrow")
    wides, narrows = lax.axis_size("wide"), lax.axis_size("narrow")

    def at(step_x, step_y):
        return (lax.rem(wide + step_x + wides, wides), lax.rem(narrow + step_y + narrows, narrows))

    steps = [(1, 0), (-1, 0), (0, 1), (0, -1), (1, 1), (1, -1), (-1, 1), (-1, -1)]
    barrier = pltpu.get_barrier_semaphore()
    for step in steps:
        pl.semaphore_signal(barrier, inc=1, device_id=at(*step), device_id_type=MESH)
    pl.semaphore_wait(barrier, len(steps))

    copies = []
    for index, (step_x, step_y) in enumerate(steps):
        from_x = size_x - 1 if step_x == 1 else 0
        from_y = size_y - 1 if step_y == 1 else 0
        low_x = 0 if step_x == 1 else 1
        low_y = 0 if step_y == 1 else 1
        if step_y == 0:
            source, target = cells.at[from_x], x_side.at[low_x]
        elif step_x == 0:
            source, target = cells.at[:, from_y], y_side.at[low_y]
        else:
            source, target = cells.at[from_x, from_y], corner.at[low_x, low_y]
        copy = pltpu.make_async_remote_copy(
            src_ref=source, dst_ref=target, send_sem=send_sem.at[index], recv_sem=recv_sem.at[index],
            device_id=at(step_x, step_y), device_id_type=MESH,
        )
        copy.start()
        copies.append(copy)

    q1[...] = dot(latents[...], w_q1[...]).astype(BF16)

    def widen(x, carry):
        pad[x + 1, 1 : size_y + 1] = cells[x].astype(F32)
        return carry

    lax.fori_loop(0, size_x, widen, 0)
    for copy in copies:
        copy.wait()
    for low in range(2):
        keep_x = (wide > 0) if low == 0 else (wide < wides - 1)
        keep_y = (narrow > 0) if low == 0 else (narrow < narrows - 1)
        pad[low * (size_x + 1), 1 : size_y + 1] = jnp.where(keep_x, x_side[low].astype(F32), 0.0)
        pad[1 : size_x + 1, low * (size_y + 1)] = jnp.where(keep_y, y_side[low].astype(F32), 0.0)
        for low_y in range(2):
            keep = jnp.logical_and(keep_x, (narrow > 0) if low_y == 0 else (narrow < narrows - 1))
            pad[low * (size_x + 1), low_y * (size_y + 1)] = jnp.where(keep, corner[low, low_y].astype(F32), 0.0)

    level = lax.broadcasted_iota(jnp.int32, (size_z, 128), 0)

    def plane(x, carry):
        for column in range(width // 128):
            lanes = slice(column * 128, column * 128 + 128)
            taps = [conv[tap : tap + 1, lanes] for tap in range(27)]
            for y in range(size_y):
                sums = [None, None, None]
                for a in range(3):
                    for b in range(3):
                        value = pad[x + a, y + b, :, lanes]
                        if a == 1 and b == 1:
                            centre = value
                        for c in range(3):
                            term = value * taps[9 * a + 3 * b + c]
                            sums[c] = term if sums[c] is None else sums[c] + term
                below = jnp.where(level == 0, 0.0, pltpu.roll(sums[0], 1, 0))
                above = jnp.where(level == size_z - 1, 0.0, pltpu.roll(sums[2], size_z - 1, 0))
                total = (centre + sums[1]) + (below + above)
                start = pl.multiple_of((x * size_y + y) * size_z, size_z)
                mixed[pl.ds(start, size_z), lanes] = total.astype(BF16)
        rows = pl.ds(pl.multiple_of(x * size_y * size_z, size_y * size_z), size_y * size_z)
        block = mixed[rows, :]
        k1[rows, :] = dot(block, w_k1[...]).astype(BF16)
        v1[rows, :] = dot(block, w_v1[...]).astype(BF16)
        q2[rows, :] = dot(block, w_q2[...]).astype(BF16)
        return carry

    lax.fori_loop(0, size_x, plane, 0)


def stencil_call(cells, conv, latents, w_q1, w_k1, w_v1, w_q2):
    size_x, size_y, size_z, width = cells.shape
    count = size_x * size_y * size_z
    rows = jax.ShapeDtypeStruct((count, width), BF16)
    return pl.pallas_call(
        stencil_kernel,
        out_shape=(jax.ShapeDtypeStruct(latents.shape, BF16), rows, rows, rows),
        in_specs=[vmem()] * 7,
        out_specs=[vmem()] * 4,
        scratch_shapes=[
            pltpu.VMEM((2, size_y, size_z, width), BF16),
            pltpu.VMEM((2, size_x, size_z, width), BF16),
            pltpu.VMEM((2, 2, size_z, width), BF16),
            pltpu.VMEM((size_x + 2, size_y + 2, size_z, width), F32),
            pltpu.VMEM((count, width), BF16),
            pltpu.SemaphoreType.DMA((8,)),
            pltpu.SemaphoreType.DMA((8,)),
        ],
        compiler_params=pltpu.CompilerParams(
            collective_id=0, has_side_effects=True, vmem_limit_bytes=56 * 2**20
        ),
        name="stencil",
    )(cells, conv, latents, w_q1, w_k1, w_v1, w_q2)


def pipelined(items, scores, weigh, read):
    score, weight, top, out = scores(*items[0]), None, None, {}
    for j in range(len(items) + 1):
        later = scores(*items[j + 1]) if j + 1 < len(items) else None
        fresh = weigh(score) if j < len(items) else (None, None)
        if j > 0:
            out[items[j - 1]] = read(weight, top, *items[j - 1])
        score, (weight, top) = later, fresh
    return out


def latent_kernel(
    scale, block,
    q1, k1, v1, latents, w_o1, w_k2, w_v2,
    k2, v2,
    part, stat, part_in, stat_in, group, group_in, own, gathered, wide_read,
    send_part, recv_part, send_stat, recv_stat, send_group, recv_group,
    send_own, recv_own, send_read, recv_read,
):
    count, width = q1.shape
    cell_count = k1.shape[0]
    pairs = width // 128
    wide, narrow = lax.axis_index("wide"), lax.axis_index("narrow")
    narrows = lax.axis_size("narrow")
    inner = 8
    outer = lax.axis_size("wide") // inner * narrows
    slice_rows = count // inner
    own_rows = slice_rows // outer
    floor = wide // inner
    near = wide - floor * inner
    far = floor * narrows + narrow

    def near_device(step):
        return (floor * inner + lax.rem(near + step, inner), narrow)

    def far_device(step):
        place = lax.rem(far + step, outer)
        return ((place // narrows) * inner + near, lax.rem(place, narrows))

    barrier = pltpu.get_barrier_semaphore()

    def greet_near(step, carry):
        pl.semaphore_signal(barrier, inc=1, device_id=near_device(step), device_id_type=MESH)
        return carry

    def greet_far(step, carry):
        pl.semaphore_signal(barrier, inc=1, device_id=far_device(step), device_id_type=MESH)
        return carry

    lax.fori_loop(1, inner, greet_near, 0)
    lax.fori_loop(1, outer, greet_far, 0)

    lane = lax.broadcasted_iota(jnp.int32, (1, 128), 1)
    level = lax.broadcasted_iota(jnp.int32, (8, 128), 0)

    def attend(pair):
        columns = pl.ds(pl.multiple_of(pair * 128, 128), 128)
        keys = k1[:, columns]
        values = jnp.concatenate([v1[:, columns], jnp.ones((cell_count, 128), BF16)], axis=1)

        def scores(start, half):
            rows = q1[start : start + block, columns]
            return dot_t(jnp.where(lane // 64 == half, rows, BF16(0)), keys)

        def weigh(score):
            top = jnp.max(score, axis=1, keepdims=True)
            return jnp.exp2((score - top) * scale).astype(BF16), top

        def read(weight, top, start, half):
            summed = dot(weight, values)
            return summed[:, :128] / summed[:, 128:], top * scale + jnp.log2(summed[:, 128:])

        items = [(start, half) for start in range(0, count, block) for half in range(2)]
        out = pipelined(items, scores, weigh, read)
        for start in range(0, count, block):
            (first, first_log), (second, second_log) = out[(start, 0)], out[(start, 1)]
            part[pair, start : start + block, :] = jnp.where(lane < 64, first, second).astype(BF16)
            logs = jnp.where(lane < 64, first_log, second_log)
            for begin in range(0, block, slice_rows):
                turned = jnp.transpose(logs[begin : begin + slice_rows, :])
                stat[pair, (start + begin) // slice_rows] = jnp.where(level < 4, turned[0:8], turned[64:72])

    def send_first(pair):
        def send(step, carry):
            place = lax.rem(near + step, inner)
            rows = pl.ds(pl.multiple_of(place * slice_rows, slice_rows), slice_rows)
            pltpu.make_async_remote_copy(
                src_ref=part.at[pair, rows], dst_ref=part_in.at[pair, step],
                send_sem=send_part.at[pair], recv_sem=recv_part.at[pair],
                device_id=near_device(step), device_id_type=MESH,
            ).start()
            pltpu.make_async_remote_copy(
                src_ref=stat.at[pair, place], dst_ref=stat_in.at[pair, step],
                send_sem=send_stat.at[pair], recv_sem=recv_stat.at[pair],
                device_id=near_device(step), device_id_type=MESH,
            ).start()
            return carry

        lax.fori_loop(1, inner, send, 0)

    def wait_for(ref, semaphore):
        pltpu.make_async_copy(ref, ref, semaphore).wait()

    def merge_first(pair):
        wait_for(part_in.at[pair, 1:inner], recv_part.at[pair])
        wait_for(stat_in.at[pair, 1:inner], recv_stat.at[pair])
        rows = pl.ds(pl.multiple_of(near * slice_rows, slice_rows), slice_rows)
        stats = [stat[pair, near]] + [stat_in[pair, step] for step in range(1, inner)]
        turned = jnp.transpose(jnp.concatenate(stats + [jnp.zeros((128 - 8 * inner, 128), F32)], axis=0))
        logs = [
            jnp.where(lane < 64, turned[:, 8 * step : 8 * step + 1], turned[:, 8 * step + 4 : 8 * step + 5])
            for step in range(inner)
        ]
        top = functools.reduce(jnp.maximum, logs)
        summed, total = 0.0, 0.0
        for step in range(inner):
            weight = jnp.exp2(logs[step] - top)
            source = part[pair, rows, :] if step == 0 else part_in[pair, step]
            summed = summed + weight * source.astype(F32)
            total = total + weight
        group[pair, :, :own_rows, :] = (summed / total).reshape(outer, own_rows, 128)
        group[pair, :, own_rows:, :] = (top + jnp.log2(total)).reshape(outer, own_rows, 128)

        def send(step, carry):
            place = lax.rem(far + step, outer)
            pltpu.make_async_remote_copy(
                src_ref=group.at[pair, place], dst_ref=group_in.at[pair, step],
                send_sem=send_group.at[pair], recv_sem=recv_group.at[pair],
                device_id=far_device(step), device_id_type=MESH,
            ).start()
            return carry

        lax.fori_loop(1, outer, send, 0)

    def merge_second(pair):
        wait_for(group_in.at[pair, 1:outer], recv_group.at[pair])
        blocks = [group[pair, far]] + [group_in[pair, step] for step in range(1, outer)]
        logs = [piece[own_rows:] for piece in blocks]
        top = functools.reduce(jnp.maximum, logs)
        summed, total = 0.0, 0.0
        for step in range(outer):
            weight = jnp.exp2(logs[step] - top)
            summed = summed + weight * blocks[step][:own_rows]
            total = total + weight
        own[pair, far] = summed / total

        def send(step, carry):
            pltpu.make_async_remote_copy(
                src_ref=own.at[pair, far], dst_ref=own.at[pair, far],
                send_sem=send_own.at[pair], recv_sem=recv_own.at[pair],
                device_id=far_device(step), device_id_type=MESH,
            ).start()
            return carry

        lax.fori_loop(1, outer, send, 0)

    def spread(pair):
        wait_for(own.at[pair, 1:outer], recv_own.at[pair])
        gathered[pair, near] = own[pair].reshape(slice_rows, 128).astype(BF16)

        def send(step, carry):
            pltpu.make_async_remote_copy(
                src_ref=gathered.at[pair, near], dst_ref=gathered.at[pair, near],
                send_sem=send_read.at[pair], recv_sem=recv_read.at[pair],
                device_id=near_device(step), device_id_type=MESH,
            ).start()
            return carry

        lax.fori_loop(1, inner, send, 0)

    def turn(step, carry):
        @pl.when(step < pairs)
        def _():
            attend(step)

        @pl.when(step == 0)
        def _():
            pl.semaphore_wait(barrier, inner + outer - 2)

        @pl.when(step < pairs)
        def _():
            send_first(step)

        @pl.when(jnp.logical_and(step >= 1, step < pairs + 1))
        def _():
            merge_first(step - 1)

        @pl.when(jnp.logical_and(step >= 2, step < pairs + 2))
        def _():
            merge_second(step - 2)

        @pl.when(step >= 3)
        def _():
            spread(step - 3)

        return carry

    lax.fori_loop(0, pairs + 3, turn, 0)

    for pair in range(pairs):
        wait_for(gathered.at[pair, 1:inner], recv_read.at[pair])
        wide_read[:, pair * 128 : pair * 128 + 128] = gathered[pair].reshape(count, 128)
    state = (latents[...].astype(F32) + dot(wide_read[...], w_o1[...])).astype(BF16)
    k2[...] = dot(state, w_k2[...]).astype(BF16)
    v2[...] = dot(state, w_v2[...]).astype(BF16)
    for pair in range(pairs):
        wait_for(part_in.at[pair, 1:inner], send_part.at[pair])
        wait_for(stat_in.at[pair, 1:inner], send_stat.at[pair])
        wait_for(group_in.at[pair, 1:outer], send_group.at[pair])
        wait_for(own.at[pair, 1:outer], send_own.at[pair])
        wait_for(gathered.at[pair, 1:inner], send_read.at[pair])


def latent_call(scale, q1, k1, v1, latents, w_o1, w_k2, w_v2):
    count, width = q1.shape
    pairs = width // 128
    inner = 8
    outer = lax.axis_size("wide") // inner * lax.axis_size("narrow")
    slice_rows = count // inner
    own_rows = slice_rows // outer
    rows = jax.ShapeDtypeStruct((count, width), BF16)
    return pl.pallas_call(
        functools.partial(latent_kernel, scale, 256),
        out_shape=(rows, rows),
        in_specs=[vmem()] * 7,
        out_specs=[vmem()] * 2,
        scratch_shapes=[
            pltpu.VMEM((pairs, count, 128), BF16),
            pltpu.VMEM((pairs, inner, 8, 128), F32),
            pltpu.VMEM((pairs, inner, slice_rows, 128), BF16),
            pltpu.VMEM((pairs, inner, 8, 128), F32),
            pltpu.VMEM((pairs, outer, 2 * own_rows, 128), F32),
            pltpu.VMEM((pairs, outer, 2 * own_rows, 128), F32),
            pltpu.VMEM((pairs, outer, own_rows, 128), F32),
            pltpu.VMEM((pairs, inner, slice_rows, 128), BF16),
            pltpu.VMEM((count, width), BF16),
        ]
        + [pltpu.SemaphoreType.DMA((pairs,))] * 10,
        compiler_params=pltpu.CompilerParams(
            collective_id=1, has_side_effects=True, vmem_limit_bytes=56 * 2**20
        ),
        name="latents",
    )(q1, k1, v1, latents, w_o1, w_k2, w_v2)


def cell_kernel(scale, q2, k2, v2, cells, w_o2, out):
    count = k2.shape[0]
    heads = q2.shape[1] // 64
    lane = lax.broadcasted_iota(jnp.int32, (1, 128), 1)
    ones = jnp.ones((count, 128), BF16)

    def columns(head):
        return slice(head // 2 * 128, head // 2 * 128 + 128)

    def scores(head):
        return dot_t(jnp.where(lane // 64 == head % 2, q2[:, columns(head)], BF16(0)), k2[:, columns(head)])

    def weigh(score):
        top = jnp.max(score, axis=1, keepdims=True)
        return jnp.exp2((score - top) * scale).astype(BF16), None

    def read(weight, top, head):
        summed = dot(weight, jnp.concatenate([v2[:, columns(head)], ones], axis=1))
        return summed[:, :128] / summed[:, 128:]

    found = pipelined([(head,) for head in range(heads)], scores, weigh, read)
    reads = [
        jnp.where(lane < 64, found[(head,)], found[(head + 1,)]).astype(BF16) for head in range(0, heads, 2)
    ]
    out[...] = cells[...].astype(F32) + dot(jnp.concatenate(reads, axis=1), w_o2[...])


def cell_call(scale, q2, k2, v2, cells, w_o2):
    count, width = q2.shape
    block = 512
    by_rows = pl.BlockSpec((block, width), lambda step: (step, 0))

    def whole(array):
        return pl.BlockSpec(array.shape, lambda step: (0, 0))

    return pl.pallas_call(
        functools.partial(cell_kernel, scale),
        out_shape=jax.ShapeDtypeStruct((count, width), F32),
        grid=(count // block,),
        in_specs=[by_rows, whole(k2), whole(v2), by_rows, whole(w_o2)],
        out_specs=by_rows,
        compiler_params=pltpu.CompilerParams(vmem_limit_bytes=56 * 2**20),
        name="cells",
    )(q2, k2, v2, cells, w_o2)


def per_device(
    flow_field, fluid_mask, conv_weight, latents,
    w_query1, w_key1, w_value1, w_out1, w_query2, w_key2, w_value2, w_out2,
):
    size_x, size_y, size_z, width = flow_field.shape
    scale = 1.8 / math.sqrt(width // HEADS) * math.log2(math.e)
    masked = flow_field * fluid_mask[:, :, :, None].astype(BF16)
    q1, k1, v1, q2 = stencil_call(masked, conv_weight, latents, w_query1, w_key1, w_value1, w_query2)
    k2, v2 = latent_call(scale, q1, k1, v1, latents, w_out1, w_key2, w_value2)
    flat = masked.reshape(size_x * size_y * size_z, width)
    result = cell_call(scale, q2, k2, v2, flat, w_out2)
    return result.reshape(size_x, size_y, size_z, width)


def solution(mesh):
    cells = P("wide", "narrow", None, None)
    return jax.shard_map(
        per_device,
        mesh=mesh,
        in_specs=(cells, P("wide", "narrow", None)) + (P(),) * 10,
        out_specs=cells,
        check_vma=False,
    )
```

```python
import functools
import math

import jax
import jax.numpy as jnp
from jax import lax
from jax.experimental import pallas as pl
from jax.experimental.pallas import tpu as pltpu
from jax.sharding import PartitionSpec as P

HEADS = 8
MESH = pl.DeviceIdType.MESH
F32 = jnp.float32
BF16 = jnp.bfloat16


def dot(a, b):
    return jnp.dot(a, b, preferred_element_type=F32)


def dot_t(a, b):
    return lax.dot_general(a, b, (((1,), (1,)), ((), ())), preferred_element_type=F32)


def mask_rows(plane):
    size_y, size_z = plane.shape
    row = lax.broadcasted_iota(jnp.int32, (size_y * size_z, size_y), 0)
    column = lax.broadcasted_iota(jnp.int32, (size_y * size_z, size_y), 1)
    spread = dot((row // size_z == column).astype(F32).astype(BF16), plane.astype(F32).astype(BF16))
    row = lax.broadcasted_iota(jnp.int32, (size_y * size_z, size_z), 0)
    column = lax.broadcasted_iota(jnp.int32, (size_y * size_z, size_z), 1)
    picked = jnp.where(row % size_z == column, spread, 0.0).astype(BF16)
    return dot(picked, jnp.ones((size_z, 128), BF16)).astype(BF16)


def vmem():
    return pl.BlockSpec(memory_space=pltpu.VMEM)


def pipelined(items, scores, weigh, read):
    score, weight, top, out = scores(*items[0]), None, None, {}
    for j in range(len(items) + 1):
        later = scores(*items[j + 1]) if j + 1 < len(items) else None
        fresh = weigh(score) if j < len(items) else (None, None)
        if j > 0:
            out[items[j - 1]] = read(weight, top, *items[j - 1])
        score, (weight, top) = later, fresh
    return out


def layer_kernel(
    scale, chunks,
    cells, mask, conv, latents, w_q1, w_k1, w_v1, w_o1, w_q2, w_k2, w_v2,
    out,
    masked, x_side, y_side, corner, pad, taps, mixed, q1, k1, v1, q2,
    part, stat, part_in, stat_in, group, group_in, own, gathered, sums, tops,
    send_side, recv_side,
    send_part, recv_part, send_stat, recv_stat, send_group, recv_group,
    send_own, recv_own, send_read, recv_read,
):
    size_x, size_y, size_z, width = cells.shape
    plane_cells = size_y * size_z
    cell_count = size_x * plane_cells
    block = latents.shape[0] // chunks
    pairs = width // 128
    wide, narrow = lax.axis_index("wide"), lax.axis_index("narrow")
    wides, narrows = lax.axis_size("wide"), lax.axis_size("narrow")
    inner = 8
    outer = wides // inner * narrows
    slice_rows = block * pairs // inner
    own_rows = slice_rows // outer
    floor = wide // inner
    near = wide - floor * inner
    far = floor * narrows + narrow

    def near_device(step):
        return (floor * inner + lax.rem(near + step, inner), narrow)

    def far_device(step):
        place = lax.rem(far + step, outer)
        return ((place // narrows) * inner + near, lax.rem(place, narrows))

    def beside(step_x, step_y):
        return (lax.rem(wide + step_x + wides, wides), lax.rem(narrow + step_y + narrows, narrows))

    barrier = pltpu.get_barrier_semaphore()
    steps = [(1, 0), (-1, 0), (0, 1), (0, -1), (1, 1), (1, -1), (-1, 1), (-1, -1)]

    def greet_near(step, carry):
        pl.semaphore_signal(barrier, inc=1, device_id=near_device(step), device_id_type=MESH)
        return carry

    def greet_far(step, carry):
        pl.semaphore_signal(barrier, inc=1, device_id=far_device(step), device_id_type=MESH)
        return carry

    for step in steps:
        pl.semaphore_signal(barrier, inc=1, device_id=beside(*step), device_id_type=MESH)
    lax.fori_loop(1, outer, greet_far, 0)
    lax.fori_loop(1, inner, greet_near, 0)

    lane = lax.broadcasted_iota(jnp.int32, (1, 128), 1)
    level = lax.broadcasted_iota(jnp.int32, (8, 128), 0)

    def columns(pair):
        return slice(pair * 128, pair * 128 + 128)

    def cover(x, carry):
        fluid = jnp.concatenate([mask_rows(mask[x])] * pairs, axis=1)
        plane = (cells[x].reshape(plane_cells, width) * fluid).reshape(size_y, size_z, width)
        masked[x] = plane
        pad[x + 1, 1 : size_y + 1] = plane.astype(F32)
        return carry

    lax.fori_loop(0, size_x, cover, 0)
    for tap in range(27):
        taps[tap] = jnp.broadcast_to(conv[tap : tap + 1, :], (8, width))

    pl.semaphore_wait(barrier, inner + outer - 2 + len(steps))
    copies = []
    for index, (step_x, step_y) in enumerate(steps):
        from_x = size_x - 1 if step_x == 1 else 0
        from_y = size_y - 1 if step_y == 1 else 0
        low_x = 0 if step_x == 1 else 1
        low_y = 0 if step_y == 1 else 1
        if step_y == 0:
            source, target = masked.at[from_x], x_side.at[low_x]
        elif step_x == 0:
            source, target = masked.at[:, from_y], y_side.at[low_y]
        else:
            source, target = masked.at[from_x, from_y], corner.at[low_x, low_y]
        copy = pltpu.make_async_remote_copy(
            src_ref=source, dst_ref=target, send_sem=send_side.at[index], recv_sem=recv_side.at[index],
            device_id=beside(step_x, step_y), device_id_type=MESH,
        )
        copy.start()
        copies.append(copy)

    depth = lax.broadcasted_iota(jnp.int32, (size_z, 128), 0)

    def strip(x, column, first, last):
        lanes = columns(column)
        found = {}
        centre = {}
        for y in range(first - 1, last + 1):
            for a in range(3):
                value = pad[x + a, y + 1, :, lanes].reshape(size_z // 8, 8, 128)
                for b in range(3):
                    target = y + 1 - b
                    if not first <= target < last:
                        continue
                    if a == 1 and b == 1:
                        centre[target] = value
                    for c in range(3):
                        term = value * taps[9 * a + 3 * b + c, :, lanes]
                        key = (target, c)
                        found[key] = found[key] + term if key in found else term
            target = y - 1
            if first <= target < last:
                low, mid, high = [found.pop((target, c)).reshape(size_z, 128) for c in range(3)]
                below = jnp.where(depth == 0, 0.0, pltpu.roll(low, 1, 0))
                above = jnp.where(depth == size_z - 1, 0.0, pltpu.roll(high, size_z - 1, 0))
                total = (centre.pop(target).reshape(size_z, 128) + mid) + (below + above)
                start = pl.multiple_of((x * size_y + target) * size_z, size_z)
                mixed[pl.ds(start, size_z), lanes] = total.astype(BF16)

    def middle(x, carry):
        for column in range(pairs):
            strip(x, column, 1, size_y - 1)
        return carry

    lax.fori_loop(1, size_x - 1, middle, 0)
    q1[...] = dot(latents[...], w_q1[...]).astype(BF16)

    for copy in copies:
        copy.wait()
    for low in range(2):
        keep_x = (wide > 0) if low == 0 else (wide < wides - 1)
        keep_y = (narrow > 0) if low == 0 else (narrow < narrows - 1)
        pad[low * (size_x + 1), 1 : size_y + 1] = jnp.where(keep_x, x_side[low].astype(F32), 0.0)
        pad[1 : size_x + 1, low * (size_y + 1)] = jnp.where(keep_y, y_side[low].astype(F32), 0.0)
        for low_y in range(2):
            keep = jnp.logical_and(keep_x, (narrow > 0) if low_y == 0 else (narrow < narrows - 1))
            pad[low * (size_x + 1), low_y * (size_y + 1)] = jnp.where(keep, corner[low, low_y].astype(F32), 0.0)

    def ends(side, carry):
        for column in range(pairs):
            strip(side * (size_x - 1), column, 0, size_y)
        return carry

    def edges(x, carry):
        for column in range(pairs):
            strip(x, column, 0, 1)
            strip(x, column, size_y - 1, size_y)
        return carry

    lax.fori_loop(0, 2, ends, 0)
    lax.fori_loop(1, size_x - 1, edges, 0)

    tall = cell_count // 4

    def project_first(step, carry):
        rows = pl.ds(pl.multiple_of(step * tall, tall), tall)
        k1[rows, :] = dot(mixed[rows, :], w_k1[...]).astype(BF16)
        v1[rows, :] = dot(mixed[rows, :], w_v1[...]).astype(BF16)
        return carry

    def project_second(step, carry):
        rows = pl.ds(pl.multiple_of(step * tall, tall), tall)
        q2[rows, :] = dot(mixed[rows, :], w_q2[...]).astype(BF16)
        return carry

    lax.fori_loop(0, 4, project_first, 0)

    def attend(chunk):
        rows = pl.ds(pl.multiple_of(chunk * block, block), block)

        def scores(pair, half):
            return dot_t(jnp.where(lane // 64 == half, q1[rows, columns(pair)], BF16(0)), k1[:, columns(pair)])

        def weigh(score):
            top = jnp.max(score, axis=1, keepdims=True)
            return jnp.exp2((score - top) * scale).astype(BF16), top

        def read(weight, top, pair, half):
            values = jnp.concatenate([v1[:, columns(pair)], jnp.ones((cell_count, 128), BF16)], axis=1)
            summed = dot(weight, values)
            return summed[:, :128] / summed[:, 128:], top * scale + jnp.log2(summed[:, 128:])

        items = [(pair, half) for pair in range(pairs) for half in range(2)]
        found = pipelined(items, scores, weigh, read)
        for pair in range(pairs):
            (first, first_log), (second, second_log) = found[(pair, 0)], found[(pair, 1)]
            start = pair * block
            part[chunk, start : start + block, :] = jnp.where(lane < 64, first, second).astype(BF16)
            logs = jnp.where(lane < 64, first_log, second_log)
            for begin in range(0, block, slice_rows):
                turned = jnp.transpose(logs[begin : begin + slice_rows, :])
                stat[chunk, (start + begin) // slice_rows] = jnp.where(level < 4, turned[0:8], turned[64:72])

    def send_first(chunk):
        def send(step, carry):
            place = lax.rem(near + step, inner)
            rows = pl.ds(pl.multiple_of(place * slice_rows, slice_rows), slice_rows)
            pltpu.make_async_remote_copy(
                src_ref=part.at[chunk, rows], dst_ref=part_in.at[chunk, step],
                send_sem=send_part.at[chunk], recv_sem=recv_part.at[chunk],
                device_id=near_device(step), device_id_type=MESH,
            ).start()
            pltpu.make_async_remote_copy(
                src_ref=stat.at[chunk, place], dst_ref=stat_in.at[chunk, step],
                send_sem=send_stat.at[chunk], recv_sem=recv_stat.at[chunk],
                device_id=near_device(step), device_id_type=MESH,
            ).start()
            return carry

        lax.fori_loop(1, inner, send, 0)

    def wait_for(ref, semaphore):
        pltpu.make_async_copy(ref, ref, semaphore).wait()

    def merge_first(chunk):
        wait_for(part_in.at[chunk, 1:inner], recv_part.at[chunk])
        wait_for(stat_in.at[chunk, 1:inner], recv_stat.at[chunk])
        rows = pl.ds(pl.multiple_of(near * slice_rows, slice_rows), slice_rows)
        stats = [stat[chunk, near]] + [stat_in[chunk, step] for step in range(1, inner)]
        turned = jnp.transpose(jnp.concatenate(stats + [jnp.zeros((128 - 8 * inner, 128), F32)], axis=0))
        logs = [
            jnp.where(lane < 64, turned[:, 8 * step : 8 * step + 1], turned[:, 8 * step + 4 : 8 * step + 5])
            for step in range(inner)
        ]
        top = functools.reduce(jnp.maximum, logs)
        summed, total = 0.0, 0.0
        for step in range(inner):
            weight = jnp.exp2(logs[step] - top)
            source = part[chunk, rows, :] if step == 0 else part_in[chunk, step]
            summed = summed + weight * source.astype(F32)
            total = total + weight
        group[chunk, :, :own_rows, :] = (summed / total).reshape(outer, own_rows, 128)
        group[chunk, :, own_rows:, :] = (top + jnp.log2(total)).reshape(outer, own_rows, 128)

        def send(step, carry):
            place = lax.rem(far + step, outer)
            pltpu.make_async_remote_copy(
                src_ref=group.at[chunk, place], dst_ref=group_in.at[chunk, step],
                send_sem=send_group.at[chunk], recv_sem=recv_group.at[chunk],
                device_id=far_device(step), device_id_type=MESH,
            ).start()
            return carry

        lax.fori_loop(1, outer, send, 0)

    def merge_second(chunk):
        wait_for(group_in.at[chunk, 1:outer], recv_group.at[chunk])
        blocks = [group[chunk, far]] + [group_in[chunk, step] for step in range(1, outer)]
        logs = [piece[own_rows:] for piece in blocks]
        top = functools.reduce(jnp.maximum, logs)
        summed, total = 0.0, 0.0
        for step in range(outer):
            weight = jnp.exp2(logs[step] - top)
            summed = summed + weight * blocks[step][:own_rows]
            total = total + weight
        own[chunk, far] = summed / total

        def send(step, carry):
            pltpu.make_async_remote_copy(
                src_ref=own.at[chunk, far], dst_ref=own.at[chunk, far],
                send_sem=send_own.at[chunk], recv_sem=recv_own.at[chunk],
                device_id=far_device(step), device_id_type=MESH,
            ).start()
            return carry

        lax.fori_loop(1, outer, send, 0)

    def spread(chunk):
        wait_for(own.at[chunk, 1:outer], recv_own.at[chunk])
        gathered[chunk, near] = own[chunk].reshape(slice_rows, 128).astype(BF16)

        def send(step, carry):
            pltpu.make_async_remote_copy(
                src_ref=gathered.at[chunk, near], dst_ref=gathered.at[chunk, near],
                send_sem=send_read.at[chunk], recv_sem=recv_read.at[chunk],
                device_id=near_device(step), device_id_type=MESH,
            ).start()
            return carry

        lax.fori_loop(1, inner, send, 0)

    def turn(step, carry):
        attend(step)
        send_first(step)

        @pl.when(step >= 3)
        def _():
            spread(step - 3)

        @pl.when(step >= 2)
        def _():
            merge_second(step - 2)

        @pl.when(step >= 1)
        def _():
            merge_first(step - 1)

        return carry

    lax.fori_loop(0, chunks, turn, 0)

    def latent_side(chunk):
        wait_for(gathered.at[chunk, 1:inner], recv_read.at[chunk])
        every = gathered[chunk].reshape(pairs, block, 128)
        read1 = jnp.concatenate([every[pair] for pair in range(pairs)], axis=1)
        rows = slice(chunk * block, chunk * block + block)
        state = (latents[rows, :].astype(F32) + dot(read1, w_o1[...])).astype(BF16)
        return dot(state, w_k2[...]).astype(BF16), dot(state, w_v2[...]).astype(BF16)

    high = cell_count // 2

    def absorb(part_index, keys, values, between):
        last = part_index == 1
        span = keys.shape[0]

        def rows_of(step, carry):
            rows = pl.ds(pl.multiple_of(step * high, high), high)

            def scores(pair, half):
                return dot_t(jnp.where(lane // 64 == half, q2[rows, columns(pair)], BF16(0)), keys[:, columns(pair)])

            def update(score, pair, half):
                top = jnp.max(score, axis=1, keepdims=True)
                shrink = None
                if last:
                    before = tops[2 * pair + half, rows, :]
                    top = jnp.maximum(before, top)
                    shrink = jnp.exp2((before - top) * scale)
                    top = jnp.concatenate([top] * (span // 128), axis=1)
                else:
                    tops[2 * pair + half, rows, :] = jnp.broadcast_to(top, (high, 128))
                return jnp.exp2((score - top) * scale).astype(BF16), shrink

            def add(weight, shrink, pair, half):
                both = jnp.where(lane // 64 == half, values[:, columns(pair)], BF16(1))
                summed = dot(weight, both)
                if not last:
                    sums[2 * pair + half, rows, :] = summed
                    return None
                summed = summed + shrink * sums[2 * pair + half, rows, :]
                return summed / pltpu.roll(summed, 64, 1)

            items = [(pair, half) for pair in range(pairs) for half in range(2)]
            score, weight, shrink, found = scores(*items[0]), None, None, {}
            for j in range(len(items) + 1):
                later = scores(*items[j + 1]) if j + 1 < len(items) else None
                new = update(score, *items[j]) if j < len(items) else (None, None)
                if j > 0:
                    found[items[j - 1]] = add(weight, shrink, *items[j - 1])
                    if last and items[j - 1][1] == 1:
                        pair = items[j - 1][0]
                        joined = jnp.where(lane < 64, found[(pair, 0)], found[(pair, 1)])
                        out[rows, columns(pair)] = joined.astype(BF16)
                score, (weight, shrink) = later, new
            if between is not None:

                @pl.when(step == 0)
                def _():
                    between()

            return carry

        lax.fori_loop(0, 2, rows_of, 0)

    lax.fori_loop(0, 4, project_second, 0)
    spread(chunks - 3)
    merge_second(chunks - 2)
    merge_first(chunks - 1)
    early = [latent_side(0)]
    spread(chunks - 2)
    early.append(latent_side(1))
    merge_second(chunks - 1)
    absorb(
        0,
        jnp.concatenate([keys for keys, _ in early], axis=0),
        jnp.concatenate([values for _, values in early], axis=0),
        lambda: spread(chunks - 1),
    )
    late = [latent_side(2), latent_side(3)]
    absorb(
        1,
        jnp.concatenate([keys for keys, _ in late], axis=0),
        jnp.concatenate([values for _, values in late], axis=0),
        None,
    )
    for chunk in range(chunks):
        wait_for(part_in.at[chunk, 1:inner], send_part.at[chunk])
        wait_for(stat_in.at[chunk, 1:inner], send_stat.at[chunk])
        wait_for(group_in.at[chunk, 1:outer], send_group.at[chunk])
        wait_for(own.at[chunk, 1:outer], send_own.at[chunk])
        wait_for(gathered.at[chunk, 1:inner], send_read.at[chunk])


def layer_call(scale, cells, mask, conv, latents, *weights):
    chunks = 4
    size_x, size_y, size_z, width = cells.shape
    count = size_x * size_y * size_z
    rows = latents.shape[0] // chunks * (width // 128)
    inner = 8
    outer = lax.axis_size("wide") // inner * lax.axis_size("narrow")
    slice_rows = rows // inner
    own_rows = slice_rows // outer
    return pl.pallas_call(
        functools.partial(layer_kernel, scale, chunks),
        out_shape=jax.ShapeDtypeStruct((count, width), BF16),
        in_specs=[vmem()] * 11,
        out_specs=vmem(),
        scratch_shapes=[
            pltpu.VMEM(cells.shape, BF16),
            pltpu.VMEM((2, size_y, size_z, width), BF16),
            pltpu.VMEM((2, size_x, size_z, width), BF16),
            pltpu.VMEM((2, 2, size_z, width), BF16),
            pltpu.VMEM((size_x + 2, size_y + 2, size_z, width), F32),
            pltpu.VMEM((27, 8, width), F32),
            pltpu.VMEM((count, width), BF16),
            pltpu.VMEM(latents.shape, BF16),
            pltpu.VMEM((count, width), BF16),
            pltpu.VMEM((count, width), BF16),
            pltpu.VMEM((count, width), BF16),
            pltpu.VMEM((chunks, rows, 128), BF16),
            pltpu.VMEM((chunks, inner, 8, 128), F32),
            pltpu.VMEM((chunks, inner, slice_rows, 128), BF16),
            pltpu.VMEM((chunks, inner, 8, 128), F32),
            pltpu.VMEM((chunks, outer, 2 * own_rows, 128), F32),
            pltpu.VMEM((chunks, outer, 2 * own_rows, 128), F32),
            pltpu.VMEM((chunks, outer, own_rows, 128), F32),
            pltpu.VMEM((chunks, inner, slice_rows, 128), BF16),
            pltpu.VMEM((width // 64, count, 128), F32),
            pltpu.VMEM((width // 64, count, 128), F32),
        ]
        + [pltpu.SemaphoreType.DMA((8,))] * 2
        + [pltpu.SemaphoreType.DMA((chunks,))] * 10,
        compiler_params=pltpu.CompilerParams(
            collective_id=0, has_side_effects=True, vmem_limit_bytes=62 * 2**20
        ),
        name="layer",
    )(cells, mask, conv, latents, *weights)


def project_kernel(read2, cells, mask, w_o2, out):
    width = read2.shape[1]
    planes = mask.shape[0]
    fluid = jnp.concatenate([mask_rows(mask[x]) for x in range(planes)], axis=0)
    masked = cells[...] * jnp.concatenate([fluid] * (width // 128), axis=1)
    out[...] = masked.astype(F32) + dot(read2[...], w_o2[...])


def project_call(read2, cells, mask, w_o2):
    count, width = read2.shape
    size_x, size_y, size_z = mask.shape
    planes = 2
    by_rows = pl.BlockSpec((planes * size_y * size_z, width), lambda step: (step, 0))
    return pl.pallas_call(
        project_kernel,
        out_shape=jax.ShapeDtypeStruct((count, width), F32),
        grid=(size_x // planes,),
        in_specs=[
            by_rows,
            by_rows,
            pl.BlockSpec((planes, size_y, size_z), lambda step: (step, 0, 0)),
            pl.BlockSpec(w_o2.shape, lambda step: (0, 0)),
        ],
        out_specs=by_rows,
        compiler_params=pltpu.CompilerParams(vmem_limit_bytes=32 * 2**20),
        name="project",
    )(read2, cells, mask, w_o2)


def per_device(
    flow_field, fluid_mask, conv_weight, latents,
    w_query1, w_key1, w_value1, w_out1, w_query2, w_key2, w_value2, w_out2,
):
    size_x, size_y, size_z, width = flow_field.shape
    scale = 1.8 / math.sqrt(width // HEADS) * math.log2(math.e)
    read2 = layer_call(
        scale, flow_field, fluid_mask, conv_weight, latents,
        w_query1, w_key1, w_value1, w_out1, w_query2, w_key2, w_value2,
    )
    flat = flow_field.reshape(size_x * size_y * size_z, width)
    return project_call(read2, flat, fluid_mask, w_out2).reshape(size_x, size_y, size_z, width)


def solution(mesh):
    cells = P("wide", "narrow", None, None)
    return jax.shard_map(
        per_device,
        mesh=mesh,
        in_specs=(cells, P("wide", "narrow", None)) + (P(),) * 10,
        out_specs=cells,
        check_vma=False,
    )
```

```python
import functools
import math

import jax
import jax.numpy as jnp
from jax import lax
from jax.experimental import pallas as pl
from jax.experimental.pallas import tpu as pltpu
from jax.sharding import PartitionSpec as P

HEADS = 8
MESH = pl.DeviceIdType.MESH
F32 = jnp.float32
BF16 = jnp.bfloat16


def dot(a, b):
    return jnp.dot(a, b, preferred_element_type=F32)


def dot_t(a, b):
    return lax.dot_general(a, b, (((1,), (1,)), ((), ())), preferred_element_type=F32)


def mask_rows(plane):
    size_y, size_z = plane.shape
    row = lax.broadcasted_iota(jnp.int32, (size_y * size_z, size_y), 0)
    column = lax.broadcasted_iota(jnp.int32, (size_y * size_z, size_y), 1)
    spread = dot((row // size_z == column).astype(F32).astype(BF16), plane.astype(F32).astype(BF16))
    row = lax.broadcasted_iota(jnp.int32, (size_y * size_z, size_z), 0)
    column = lax.broadcasted_iota(jnp.int32, (size_y * size_z, size_z), 1)
    picked = jnp.where(row % size_z == column, spread, 0.0).astype(BF16)
    return dot(picked, jnp.ones((size_z, 128), BF16)).astype(BF16)


def vmem():
    return pl.BlockSpec(memory_space=pltpu.VMEM)


def pipelined(items, scores, weigh, read):
    score, weight, top, out = scores(*items[0]), None, None, {}
    for j in range(len(items) + 1):
        later = scores(*items[j + 1]) if j + 1 < len(items) else None
        fresh = weigh(score) if j < len(items) else (None, None)
        if j > 0:
            out[items[j - 1]] = read(weight, top, *items[j - 1])
        score, (weight, top) = later, fresh
    return out


def layer_kernel(
    scale, chunks,
    cells, mask, conv, *rest,
):
    sources, out = rest[:9], rest[9]
    latents, w_q1, w_k1, w_v1, w_q2, w_o1, w_k2, w_v2, w_o2 = rest[10:19]
    (
    masked, x_side, y_side, corner, pad, taps, mixed, q1, k1, v1, q2,
    part, stat, part_in, stat_in, group, group_in, own, gathered, sums, tops, staged,
    send_side, recv_side,
    send_part, recv_part, send_stat, recv_stat, send_group, recv_group,
    send_own, recv_own, send_read, recv_read, load_sem, store_sem,
    ) = rest[19:]
    loads = [
        pltpu.make_async_copy(source, target, load_sem.at[index])
        for index, (source, target) in enumerate(zip(sources, rest[10:19]))
    ]
    for load in loads:
        load.start()
    size_x, size_y, size_z, width = cells.shape
    plane_cells = size_y * size_z
    cell_count = size_x * plane_cells
    block = latents.shape[0] // chunks
    pairs = width // 128
    wide, narrow = lax.axis_index("wide"), lax.axis_index("narrow")
    wides, narrows = lax.axis_size("wide"), lax.axis_size("narrow")
    inner = 8
    outer = wides // inner * narrows
    slice_rows = block * pairs // inner
    own_rows = slice_rows // outer
    floor = wide // inner
    near = wide - floor * inner
    far = floor * narrows + narrow

    def near_device(step):
        return (floor * inner + lax.rem(near + step, inner), narrow)

    def far_device(step):
        place = lax.rem(far + step, outer)
        return ((place // narrows) * inner + near, lax.rem(place, narrows))

    def beside(step_x, step_y):
        return (lax.rem(wide + step_x + wides, wides), lax.rem(narrow + step_y + narrows, narrows))

    barrier = pltpu.get_barrier_semaphore()
    steps = [(1, 0), (-1, 0), (0, 1), (0, -1), (1, 1), (1, -1), (-1, 1), (-1, -1)]

    def greet_near(step, carry):
        pl.semaphore_signal(barrier, inc=1, device_id=near_device(step), device_id_type=MESH)
        return carry

    def greet_far(step, carry):
        pl.semaphore_signal(barrier, inc=1, device_id=far_device(step), device_id_type=MESH)
        return carry

    for step in steps:
        pl.semaphore_signal(barrier, inc=1, device_id=beside(*step), device_id_type=MESH)
    lax.fori_loop(1, outer, greet_far, 0)
    lax.fori_loop(1, inner, greet_near, 0)

    lane = lax.broadcasted_iota(jnp.int32, (1, 128), 1)
    level = lax.broadcasted_iota(jnp.int32, (8, 128), 0)

    def columns(pair):
        return slice(pair * 128, pair * 128 + 128)

    def cover(x, carry):
        fluid = jnp.concatenate([mask_rows(mask[x])] * pairs, axis=1)
        plane = (cells[x].reshape(plane_cells, width) * fluid).reshape(size_y, size_z, width)
        masked[x] = plane
        pad[x + 1, 1 : size_y + 1] = plane.astype(F32)
        return carry

    lax.fori_loop(0, size_x, cover, 0)
    for tap in range(27):
        taps[tap] = jnp.broadcast_to(conv[tap : tap + 1, :], (8, width))

    pl.semaphore_wait(barrier, inner + outer - 2 + len(steps))
    copies = []
    for index, (step_x, step_y) in enumerate(steps):
        from_x = size_x - 1 if step_x == 1 else 0
        from_y = size_y - 1 if step_y == 1 else 0
        low_x = 0 if step_x == 1 else 1
        low_y = 0 if step_y == 1 else 1
        if step_y == 0:
            source, target = masked.at[from_x], x_side.at[low_x]
        elif step_x == 0:
            source, target = masked.at[:, from_y], y_side.at[low_y]
        else:
            source, target = masked.at[from_x, from_y], corner.at[low_x, low_y]
        copy = pltpu.make_async_remote_copy(
            src_ref=source, dst_ref=target, send_sem=send_side.at[index], recv_sem=recv_side.at[index],
            device_id=beside(step_x, step_y), device_id_type=MESH,
        )
        copy.start()
        copies.append(copy)

    depth = lax.broadcasted_iota(jnp.int32, (size_z, 128), 0)

    def strip(x, column, first, last):
        lanes = columns(column)
        for y in range(first, last):
            found = [None] * 3
            for a in range(3):
                for b in range(3):
                    value = pad[x + a, y + b, :, lanes].reshape(size_z // 8, 8, 128)
                    if a == 1 and b == 1:
                        centre = value
                    for c in range(3):
                        term = value * taps[9 * a + 3 * b + c, :, lanes]
                        found[c] = term if found[c] is None else found[c] + term
            centre, low, mid, high = [piece.reshape(size_z, 128) for piece in [centre] + found]
            below = jnp.where(depth == 0, 0.0, pltpu.roll(low, 1, 0))
            above = jnp.where(depth == size_z - 1, 0.0, pltpu.roll(high, size_z - 1, 0))
            start = pl.multiple_of((x * size_y + y) * size_z, size_z)
            mixed[pl.ds(start, size_z), lanes] = ((centre + mid) + (below + above)).astype(BF16)

    def middle(x, carry):
        for column in range(pairs):
            strip(x, column, 1, size_y - 1)
        return carry

    lax.fori_loop(1, size_x - 1, middle, 0)
    loads[0].wait()
    loads[1].wait()
    q1[...] = dot(latents[...], w_q1[...]).astype(BF16)

    for copy in copies:
        copy.wait()
    for low in range(2):
        keep_x = (wide > 0) if low == 0 else (wide < wides - 1)
        keep_y = (narrow > 0) if low == 0 else (narrow < narrows - 1)
        pad[low * (size_x + 1), 1 : size_y + 1] = jnp.where(keep_x, x_side[low].astype(F32), 0.0)
        pad[1 : size_x + 1, low * (size_y + 1)] = jnp.where(keep_y, y_side[low].astype(F32), 0.0)
        for low_y in range(2):
            keep = jnp.logical_and(keep_x, (narrow > 0) if low_y == 0 else (narrow < narrows - 1))
            pad[low * (size_x + 1), low_y * (size_y + 1)] = jnp.where(keep, corner[low, low_y].astype(F32), 0.0)

    def ends(side, carry):
        for column in range(pairs):
            strip(side * (size_x - 1), column, 0, size_y)
        return carry

    def edges(x, carry):
        for column in range(pairs):
            strip(x, column, 0, 1)
            strip(x, column, size_y - 1, size_y)
        return carry

    lax.fori_loop(0, 2, ends, 0)
    lax.fori_loop(1, size_x - 1, edges, 0)

    tall = cell_count // 4

    def project_first(step, carry):
        rows = pl.ds(pl.multiple_of(step * tall, tall), tall)
        k1[rows, :] = dot(mixed[rows, :], w_k1[...]).astype(BF16)
        v1[rows, :] = dot(mixed[rows, :], w_v1[...]).astype(BF16)
        return carry

    def project_second(step, carry):
        rows = pl.ds(pl.multiple_of(step * tall, tall), tall)
        q2[rows, :] = dot(mixed[rows, :], w_q2[...]).astype(BF16)
        return carry

    for load in loads[2:]:
        load.wait()
    lax.fori_loop(0, 4, project_first, 0)

    def attend(chunk):
        rows = pl.ds(pl.multiple_of(chunk * block, block), block)

        def scores(pair, half):
            return dot_t(jnp.where(lane // 64 == half, q1[rows, columns(pair)], BF16(0)), k1[:, columns(pair)])

        def weigh(score):
            top = jnp.max(score, axis=1, keepdims=True)
            return jnp.exp2((score - top) * scale).astype(BF16), top

        def read(weight, top, pair, half):
            values = jnp.concatenate([v1[:, columns(pair)], jnp.ones((cell_count, 128), BF16)], axis=1)
            summed = dot(weight, values)
            return summed[:, :128] / summed[:, 128:], top * scale + jnp.log2(summed[:, 128:])

        items = [(pair, half) for pair in range(pairs) for half in range(2)]
        found = pipelined(items, scores, weigh, read)
        for pair in range(pairs):
            (first, first_log), (second, second_log) = found[(pair, 0)], found[(pair, 1)]
            start = pair * block
            part[chunk, start : start + block, :] = jnp.where(lane < 64, first, second).astype(BF16)
            logs = jnp.where(lane < 64, first_log, second_log)
            for begin in range(0, block, slice_rows):
                turned = jnp.transpose(logs[begin : begin + slice_rows, :])
                stat[chunk, (start + begin) // slice_rows] = jnp.where(level < 4, turned[0:8], turned[64:72])

    def send_first(chunk):
        def send(step, carry):
            place = lax.rem(near + step, inner)
            rows = pl.ds(pl.multiple_of(place * slice_rows, slice_rows), slice_rows)
            pltpu.make_async_remote_copy(
                src_ref=part.at[chunk, rows], dst_ref=part_in.at[chunk, step],
                send_sem=send_part.at[chunk], recv_sem=recv_part.at[chunk],
                device_id=near_device(step), device_id_type=MESH,
            ).start()
            pltpu.make_async_remote_copy(
                src_ref=stat.at[chunk, place], dst_ref=stat_in.at[chunk, step],
                send_sem=send_stat.at[chunk], recv_sem=recv_stat.at[chunk],
                device_id=near_device(step), device_id_type=MESH,
            ).start()
            return carry

        lax.fori_loop(1, inner, send, 0)

    def wait_for(ref, semaphore):
        pltpu.make_async_copy(ref, ref, semaphore).wait()

    def merge_first(chunk):
        wait_for(part_in.at[chunk, 1:inner], recv_part.at[chunk])
        wait_for(stat_in.at[chunk, 1:inner], recv_stat.at[chunk])
        rows = pl.ds(pl.multiple_of(near * slice_rows, slice_rows), slice_rows)
        stats = [stat[chunk, near]] + [stat_in[chunk, step] for step in range(1, inner)]
        turned = jnp.transpose(jnp.concatenate(stats + [jnp.zeros((128 - 8 * inner, 128), F32)], axis=0))
        logs = [
            jnp.where(lane < 64, turned[:, 8 * step : 8 * step + 1], turned[:, 8 * step + 4 : 8 * step + 5])
            for step in range(inner)
        ]
        top = functools.reduce(jnp.maximum, logs)
        summed, total = 0.0, 0.0
        for step in range(inner):
            weight = jnp.exp2(logs[step] - top)
            source = part[chunk, rows, :] if step == 0 else part_in[chunk, step]
            summed = summed + weight * source.astype(F32)
            total = total + weight
        group[chunk, :, :own_rows, :] = (summed / total).reshape(outer, own_rows, 128)
        group[chunk, :, own_rows:, :] = (top + jnp.log2(total)).reshape(outer, own_rows, 128)

        def send(step, carry):
            place = lax.rem(far + step, outer)
            pltpu.make_async_remote_copy(
                src_ref=group.at[chunk, place], dst_ref=group_in.at[chunk, step],
                send_sem=send_group.at[chunk], recv_sem=recv_group.at[chunk],
                device_id=far_device(step), device_id_type=MESH,
            ).start()
            return carry

        lax.fori_loop(1, outer, send, 0)

    def merge_second(chunk):
        wait_for(group_in.at[chunk, 1:outer], recv_group.at[chunk])
        blocks = [group[chunk, far]] + [group_in[chunk, step] for step in range(1, outer)]
        logs = [piece[own_rows:] for piece in blocks]
        top = functools.reduce(jnp.maximum, logs)
        summed, total = 0.0, 0.0
        for step in range(outer):
            weight = jnp.exp2(logs[step] - top)
            summed = summed + weight * blocks[step][:own_rows]
            total = total + weight
        own[chunk, far] = summed / total

        def send(step, carry):
            pltpu.make_async_remote_copy(
                src_ref=own.at[chunk, far], dst_ref=own.at[chunk, far],
                send_sem=send_own.at[chunk], recv_sem=recv_own.at[chunk],
                device_id=far_device(step), device_id_type=MESH,
            ).start()
            return carry

        lax.fori_loop(1, outer, send, 0)

    def spread(chunk):
        wait_for(own.at[chunk, 1:outer], recv_own.at[chunk])
        gathered[chunk, near] = own[chunk].reshape(slice_rows, 128).astype(BF16)

        def send(step, carry):
            pltpu.make_async_remote_copy(
                src_ref=gathered.at[chunk, near], dst_ref=gathered.at[chunk, near],
                send_sem=send_read.at[chunk], recv_sem=recv_read.at[chunk],
                device_id=near_device(step), device_id_type=MESH,
            ).start()
            return carry

        lax.fori_loop(1, inner, send, 0)

    def turn(step, carry):
        attend(step)
        send_first(step)

        @pl.when(step >= 3)
        def _():
            spread(step - 3)

        @pl.when(step >= 2)
        def _():
            merge_second(step - 2)

        @pl.when(step >= 1)
        def _():
            merge_first(step - 1)

        return carry

    lax.fori_loop(0, chunks, turn, 0)

    def latent_side(chunk):
        wait_for(gathered.at[chunk, 1:inner], recv_read.at[chunk])
        every = gathered[chunk].reshape(pairs, block, 128)
        read1 = jnp.concatenate([every[pair] for pair in range(pairs)], axis=1)
        rows = slice(chunk * block, chunk * block + block)
        state = (latents[rows, :].astype(F32) + dot(read1, w_o1[...])).astype(BF16)
        return dot(state, w_k2[...]).astype(BF16), dot(state, w_v2[...]).astype(BF16)

    high = cell_count // 4

    def leave(step):
        rows = pl.ds(pl.multiple_of(step * high, high), high)
        return pltpu.make_async_copy(staged.at[step], out.at[rows], store_sem.at[step])

    def absorb(part_index, keys, values, between):
        last = part_index == 1
        span = keys.shape[0]
        per = size_x // 4

        def rows_of(step, carry):
            rows = pl.ds(pl.multiple_of(step * high, high), high)

            def scores(pair, half):
                return dot_t(jnp.where(lane // 64 == half, q2[rows, columns(pair)], BF16(0)), keys[:, columns(pair)])

            def update(score, pair, half):
                top = jnp.max(score, axis=1, keepdims=True)
                shrink = None
                if last:
                    before = tops[2 * pair + half, rows, :]
                    top = jnp.maximum(before, top)
                    shrink = jnp.exp2((before - top) * scale)
                    top = jnp.concatenate([top] * (span // 128), axis=1)
                else:
                    tops[2 * pair + half, rows, :] = jnp.broadcast_to(top, (high, 128))
                return jnp.exp2((score - top) * scale).astype(BF16), shrink

            def add(weight, shrink, pair, half):
                both = jnp.where(lane // 64 == half, values[:, columns(pair)], BF16(1))
                summed = dot(weight, both)
                if not last:
                    sums[2 * pair + half, rows, :] = summed
                    return None
                summed = summed + shrink * sums[2 * pair + half, rows, :]
                return summed / pltpu.roll(summed, 64, 1)

            items = [(pair, half) for pair in range(pairs) for half in range(2)]
            score, weight, shrink, found, joined = scores(*items[0]), None, None, {}, []
            for j in range(len(items) + 1):
                later = scores(*items[j + 1]) if j + 1 < len(items) else None
                new = update(score, *items[j]) if j < len(items) else (None, None)
                if j > 0:
                    found[items[j - 1]] = add(weight, shrink, *items[j - 1])
                    if last and items[j - 1][1] == 1:
                        pair = items[j - 1][0]
                        joined.append(jnp.where(lane < 64, found[(pair, 0)], found[(pair, 1)]).astype(BF16))
                score, (weight, shrink) = later, new
            if last:
                residual = masked[pl.ds(step * per, per)].reshape(high, width).astype(F32)
                staged[step] = residual + dot(jnp.concatenate(joined, axis=1), w_o2[...])
                leave(step).start()
            else:
                between(step)
            return carry

        lax.fori_loop(0, 4, rows_of, 0)

    lax.fori_loop(0, 4, project_second, 0)
    spread(chunks - 3)
    merge_second(chunks - 2)
    merge_first(chunks - 1)
    early = [latent_side(0), latent_side(1)]

    def between(step):
        @pl.when(step == 0)
        def _():
            spread(chunks - 2)
            merge_second(chunks - 1)

        @pl.when(step == 2)
        def _():
            spread(chunks - 1)

    absorb(
        0,
        jnp.concatenate([keys for keys, _ in early], axis=0),
        jnp.concatenate([values for _, values in early], axis=0),
        between,
    )
    late = [latent_side(2), latent_side(3)]
    absorb(
        1,
        jnp.concatenate([keys for keys, _ in late], axis=0),
        jnp.concatenate([values for _, values in late], axis=0),
        None,
    )
    for chunk in range(chunks):
        wait_for(part_in.at[chunk, 1:inner], send_part.at[chunk])
        wait_for(stat_in.at[chunk, 1:inner], send_stat.at[chunk])
        wait_for(group_in.at[chunk, 1:outer], send_group.at[chunk])
        wait_for(own.at[chunk, 1:outer], send_own.at[chunk])
        wait_for(gathered.at[chunk, 1:inner], send_read.at[chunk])
    for step in range(4):
        leave(step).wait()


def layer_call(scale, cells, mask, conv, latents, *weights):
    chunks = 4
    size_x, size_y, size_z, width = cells.shape
    count = size_x * size_y * size_z
    rows = latents.shape[0] // chunks * (width // 128)
    inner = 8
    outer = lax.axis_size("wide") // inner * lax.axis_size("narrow")
    slice_rows = rows // inner
    own_rows = slice_rows // outer
    return pl.pallas_call(
        functools.partial(layer_kernel, scale, chunks),
        out_shape=jax.ShapeDtypeStruct((count, width), F32),
        in_specs=[vmem()] * 3 + [pl.BlockSpec(memory_space=pl.ANY)] * 9,
        out_specs=pl.BlockSpec(memory_space=pl.ANY),
        scratch_shapes=[pltpu.VMEM(array.shape, array.dtype) for array in (latents, *weights)]
        + [
            pltpu.VMEM(cells.shape, BF16),
            pltpu.VMEM((2, size_y, size_z, width), BF16),
            pltpu.VMEM((2, size_x, size_z, width), BF16),
            pltpu.VMEM((2, 2, size_z, width), BF16),
            pltpu.VMEM((size_x + 2, size_y + 2, size_z, width), F32),
            pltpu.VMEM((27, 8, width), F32),
            pltpu.VMEM((count, width), BF16),
            pltpu.VMEM(latents.shape, BF16),
            pltpu.VMEM((count, width), BF16),
            pltpu.VMEM((count, width), BF16),
            pltpu.VMEM((count, width), BF16),
            pltpu.VMEM((chunks, rows, 128), BF16),
            pltpu.VMEM((chunks, inner, 8, 128), F32),
            pltpu.VMEM((chunks, inner, slice_rows, 128), BF16),
            pltpu.VMEM((chunks, inner, 8, 128), F32),
            pltpu.VMEM((chunks, outer, 2 * own_rows, 128), F32),
            pltpu.VMEM((chunks, outer, 2 * own_rows, 128), F32),
            pltpu.VMEM((chunks, outer, own_rows, 128), F32),
            pltpu.VMEM((chunks, inner, slice_rows, 128), BF16),
            pltpu.VMEM((width // 64, count, 128), F32),
            pltpu.VMEM((width // 64, count, 128), F32),
            pltpu.VMEM((4, count // 4, width), F32),
        ]
        + [pltpu.SemaphoreType.DMA((8,))] * 2
        + [pltpu.SemaphoreType.DMA((chunks,))] * 10
        + [pltpu.SemaphoreType.DMA((9,)), pltpu.SemaphoreType.DMA((4,))],
        compiler_params=pltpu.CompilerParams(
            collective_id=0, has_side_effects=True, vmem_limit_bytes=62 * 2**20
        ),
        name="layer",
    )(cells, mask, conv, latents, *weights)


def per_device(
    flow_field, fluid_mask, conv_weight, latents,
    w_query1, w_key1, w_value1, w_out1, w_query2, w_key2, w_value2, w_out2,
):
    size_x, size_y, size_z, width = flow_field.shape
    scale = 1.8 / math.sqrt(width // HEADS) * math.log2(math.e)
    result = layer_call(
        scale, flow_field, fluid_mask, conv_weight, latents,
        w_query1, w_key1, w_value1, w_query2, w_out1, w_key2, w_value2, w_out2,
    )
    return result.reshape(size_x, size_y, size_z, width)


def solution(mesh):
    cells = P("wide", "narrow", None, None)
    return jax.shard_map(
        per_device,
        mesh=mesh,
        in_specs=(cells, P("wide", "narrow", None)) + (P(),) * 10,
        out_specs=cells,
        check_vma=False,
    )
```

```python
import functools
import math

import jax
import jax.numpy as jnp
from jax import lax
from jax.experimental import pallas as pl
from jax.experimental.pallas import tpu as pltpu
from jax.sharding import PartitionSpec as P

HEADS = 8
MESH = pl.DeviceIdType.MESH
F32 = jnp.float32
BF16 = jnp.bfloat16


def dot(a, b):
    return jnp.dot(a, b, preferred_element_type=F32)


def dot_t(a, b):
    return lax.dot_general(a, b, (((1,), (1,)), ((), ())), preferred_element_type=F32)


def mask_rows(plane):
    size_y, size_z = plane.shape
    row = lax.broadcasted_iota(jnp.int32, (size_y * size_z, size_y), 0)
    column = lax.broadcasted_iota(jnp.int32, (size_y * size_z, size_y), 1)
    spread = dot((row // size_z == column).astype(F32).astype(BF16), plane.astype(F32).astype(BF16))
    row = lax.broadcasted_iota(jnp.int32, (size_y * size_z, size_z), 0)
    column = lax.broadcasted_iota(jnp.int32, (size_y * size_z, size_z), 1)
    picked = jnp.where(row % size_z == column, spread, 0.0).astype(BF16)
    return dot(picked, jnp.ones((size_z, 128), BF16)).astype(BF16)


def vmem():
    return pl.BlockSpec(memory_space=pltpu.VMEM)


def pipelined(items, scores, weigh, read):
    score, weight, top, out = scores(*items[0]), None, None, {}
    for j in range(len(items) + 1):
        later = scores(*items[j + 1]) if j + 1 < len(items) else None
        fresh = weigh(score) if j < len(items) else (None, None)
        if j > 0:
            out[items[j - 1]] = read(weight, top, *items[j - 1])
        score, (weight, top) = later, fresh
    return out


def layer_kernel(
    scale, chunks,
    cells, mask, conv, *rest,
):
    sources, out = rest[:9], rest[9]
    latents, w_q1, w_k1, w_v1, w_q2, w_o1, w_k2, w_v2, w_o2 = rest[10:19]
    (
    masked, x_side, y_side, corner, pad, taps, mixed, q1, k1, v1, q2,
    part, stat, part_in, stat_in, group, group_in, own, gathered, sums, tops,
    send_side, recv_side,
    send_part, recv_part, send_stat, recv_stat, send_group, recv_group,
    send_own, recv_own, send_read, recv_read, load_sem, store_sem,
    ) = rest[19:]
    loads = [
        pltpu.make_async_copy(source, target, load_sem.at[index])
        for index, (source, target) in enumerate(zip(sources, rest[10:19]))
    ]
    for load in loads:
        load.start()
    size_x, size_y, size_z, width = cells.shape
    plane_cells = size_y * size_z
    cell_count = size_x * plane_cells
    block = latents.shape[0] // chunks
    pairs = width // 128
    wide, narrow = lax.axis_index("wide"), lax.axis_index("narrow")
    wides, narrows = lax.axis_size("wide"), lax.axis_size("narrow")
    inner = 8
    outer = wides // inner * narrows
    slice_rows = block * pairs // inner
    own_rows = slice_rows // outer
    floor = wide // inner
    near = wide - floor * inner
    far = floor * narrows + narrow

    def near_device(step):
        return (floor * inner + lax.rem(near + step, inner), narrow)

    def far_device(step):
        place = lax.rem(far + step, outer)
        return ((place // narrows) * inner + near, lax.rem(place, narrows))

    def beside(step_x, step_y):
        return (lax.rem(wide + step_x + wides, wides), lax.rem(narrow + step_y + narrows, narrows))

    barrier = pltpu.get_barrier_semaphore()
    steps = [(1, 0), (-1, 0), (0, 1), (0, -1), (1, 1), (1, -1), (-1, 1), (-1, -1)]

    def greet_near(step, carry):
        pl.semaphore_signal(barrier, inc=1, device_id=near_device(step), device_id_type=MESH)
        return carry

    def greet_far(step, carry):
        pl.semaphore_signal(barrier, inc=1, device_id=far_device(step), device_id_type=MESH)
        return carry

    for step in steps:
        pl.semaphore_signal(barrier, inc=1, device_id=beside(*step), device_id_type=MESH)
    lax.fori_loop(1, outer, greet_far, 0)
    lax.fori_loop(1, inner, greet_near, 0)

    lane = lax.broadcasted_iota(jnp.int32, (1, 128), 1)
    level = lax.broadcasted_iota(jnp.int32, (8, 128), 0)

    def columns(pair):
        return slice(pair * 128, pair * 128 + 128)

    def cover(x, carry):
        fluid = jnp.concatenate([mask_rows(mask[x])] * pairs, axis=1)
        plane = (cells[x].reshape(plane_cells, width) * fluid).reshape(size_y, size_z, width)
        masked[x] = plane
        pad[x + 1, 1 : size_y + 1] = plane.astype(F32)
        return carry

    lax.fori_loop(0, size_x, cover, 0)
    for tap in range(27):
        taps[tap] = jnp.broadcast_to(conv[tap : tap + 1, :], (8, width))

    pl.semaphore_wait(barrier, inner + outer - 2 + len(steps))
    copies = []
    for index, (step_x, step_y) in enumerate(steps):
        from_x = size_x - 1 if step_x == 1 else 0
        from_y = size_y - 1 if step_y == 1 else 0
        low_x = 0 if step_x == 1 else 1
        low_y = 0 if step_y == 1 else 1
        if step_y == 0:
            source, target = masked.at[from_x], x_side.at[low_x]
        elif step_x == 0:
            source, target = masked.at[:, from_y], y_side.at[low_y]
        else:
            source, target = masked.at[from_x, from_y], corner.at[low_x, low_y]
        copy = pltpu.make_async_remote_copy(
            src_ref=source, dst_ref=target, send_sem=send_side.at[index], recv_sem=recv_side.at[index],
            device_id=beside(step_x, step_y), device_id_type=MESH,
        )
        copy.start()
        copies.append(copy)

    depth = lax.broadcasted_iota(jnp.int32, (size_z, 128), 0)

    def strip(x, column, first, last):
        lanes = columns(column)
        for y in range(first, last):
            found = [None] * 3
            for a in range(3):
                for b in range(3):
                    value = pad[x + a, y + b, :, lanes].reshape(size_z // 8, 8, 128)
                    if a == 1 and b == 1:
                        centre = value
                    for c in range(3):
                        term = value * taps[9 * a + 3 * b + c, :, lanes]
                        found[c] = term if found[c] is None else found[c] + term
            centre, low, mid, high = [piece.reshape(size_z, 128) for piece in [centre] + found]
            below = jnp.where(depth == 0, 0.0, pltpu.roll(low, 1, 0))
            above = jnp.where(depth == size_z - 1, 0.0, pltpu.roll(high, size_z - 1, 0))
            start = pl.multiple_of((x * size_y + y) * size_z, size_z)
            mixed[pl.ds(start, size_z), lanes] = ((centre + mid) + (below + above)).astype(BF16)

    def middle(x, carry):
        for column in range(pairs):
            strip(x, column, 1, size_y - 1)
        return carry

    lax.fori_loop(1, size_x - 1, middle, 0)
    loads[0].wait()
    loads[1].wait()
    q1[...] = dot(latents[...], w_q1[...]).astype(BF16)

    for copy in copies:
        copy.wait()
    for low in range(2):
        keep_x = (wide > 0) if low == 0 else (wide < wides - 1)
        keep_y = (narrow > 0) if low == 0 else (narrow < narrows - 1)
        pad[low * (size_x + 1), 1 : size_y + 1] = jnp.where(keep_x, x_side[low].astype(F32), 0.0)
        pad[1 : size_x + 1, low * (size_y + 1)] = jnp.where(keep_y, y_side[low].astype(F32), 0.0)
        for low_y in range(2):
            keep = jnp.logical_and(keep_x, (narrow > 0) if low_y == 0 else (narrow < narrows - 1))
            pad[low * (size_x + 1), low_y * (size_y + 1)] = jnp.where(keep, corner[low, low_y].astype(F32), 0.0)

    def ends(side, carry):
        for column in range(pairs):
            strip(side * (size_x - 1), column, 0, size_y)
        return carry

    def edges(x, carry):
        for column in range(pairs):
            strip(x, column, 0, 1)
            strip(x, column, size_y - 1, size_y)
        return carry

    lax.fori_loop(0, 2, ends, 0)
    lax.fori_loop(1, size_x - 1, edges, 0)

    tall = cell_count // 4

    def project_first(step, carry):
        rows = pl.ds(pl.multiple_of(step * tall, tall), tall)
        k1[rows, :] = dot(mixed[rows, :], w_k1[...]).astype(BF16)
        v1[rows, :] = dot(mixed[rows, :], w_v1[...]).astype(BF16)
        return carry

    def project_second(step, carry):
        rows = pl.ds(pl.multiple_of(step * tall, tall), tall)
        q2[rows, :] = dot(mixed[rows, :], w_q2[...]).astype(BF16)
        return carry

    for load in loads[2:]:
        load.wait()
    lax.fori_loop(0, 4, project_first, 0)

    def attend(chunk, first_pair, last_pair):
        rows = pl.ds(pl.multiple_of(chunk * block, block), block)

        def scores(pair, half):
            return dot_t(jnp.where(lane // 64 == half, q1[rows, columns(pair)], BF16(0)), k1[:, columns(pair)])

        def weigh(score):
            top = jnp.max(score, axis=1, keepdims=True)
            return jnp.exp2((score - top) * scale).astype(BF16), top

        def read(weight, top, pair, half):
            values = jnp.concatenate([v1[:, columns(pair)], jnp.ones((cell_count, 128), BF16)], axis=1)
            summed = dot(weight, values)
            return summed[:, :128] / summed[:, 128:], top * scale + jnp.log2(summed[:, 128:])

        items = [(pair, half) for pair in range(first_pair, last_pair) for half in range(2)]
        found = pipelined(items, scores, weigh, read)
        for pair in range(first_pair, last_pair):
            (first, first_log), (second, second_log) = found[(pair, 0)], found[(pair, 1)]
            start = pair * block
            part[chunk, start : start + block, :] = jnp.where(lane < 64, first, second).astype(BF16)
            logs = jnp.where(lane < 64, first_log, second_log)
            for begin in range(0, block, slice_rows):
                turned = jnp.transpose(logs[begin : begin + slice_rows, :])
                stat[chunk, (start + begin) // slice_rows] = jnp.where(level < 4, turned[0:8], turned[64:72])

    def send_first(chunk):
        def send(step, carry):
            place = lax.rem(near + step, inner)
            rows = pl.ds(pl.multiple_of(place * slice_rows, slice_rows), slice_rows)
            pltpu.make_async_remote_copy(
                src_ref=part.at[chunk, rows], dst_ref=part_in.at[chunk, step],
                send_sem=send_part.at[chunk], recv_sem=recv_part.at[chunk],
                device_id=near_device(step), device_id_type=MESH,
            ).start()
            pltpu.make_async_remote_copy(
                src_ref=stat.at[chunk, place], dst_ref=stat_in.at[chunk, step],
                send_sem=send_stat.at[chunk], recv_sem=recv_stat.at[chunk],
                device_id=near_device(step), device_id_type=MESH,
            ).start()
            return carry

        lax.fori_loop(1, inner, send, 0)

    def wait_for(ref, semaphore):
        pltpu.make_async_copy(ref, ref, semaphore).wait()

    def merge_first(chunk):
        wait_for(part_in.at[chunk, 1:inner], recv_part.at[chunk])
        wait_for(stat_in.at[chunk, 1:inner], recv_stat.at[chunk])
        rows = pl.ds(pl.multiple_of(near * slice_rows, slice_rows), slice_rows)
        stats = [stat[chunk, near]] + [stat_in[chunk, step] for step in range(1, inner)]
        turned = jnp.transpose(jnp.concatenate(stats + [jnp.zeros((128 - 8 * inner, 128), F32)], axis=0))
        logs = [
            jnp.where(lane < 64, turned[:, 8 * step : 8 * step + 1], turned[:, 8 * step + 4 : 8 * step + 5])
            for step in range(inner)
        ]
        top = functools.reduce(jnp.maximum, logs)
        summed, total = 0.0, 0.0
        for step in range(inner):
            weight = jnp.exp2(logs[step] - top)
            source = part[chunk, rows, :] if step == 0 else part_in[chunk, step]
            summed = summed + weight * source.astype(F32)
            total = total + weight
        group[chunk, :, :own_rows, :] = (summed / total).reshape(outer, own_rows, 128)
        group[chunk, :, own_rows:, :] = (top + jnp.log2(total)).reshape(outer, own_rows, 128)

        def send(step, carry):
            place = lax.rem(far + step, outer)
            pltpu.make_async_remote_copy(
                src_ref=group.at[chunk, place], dst_ref=group_in.at[chunk, step],
                send_sem=send_group.at[chunk], recv_sem=recv_group.at[chunk],
                device_id=far_device(step), device_id_type=MESH,
            ).start()
            return carry

        lax.fori_loop(1, outer, send, 0)

    def merge_second(chunk):
        wait_for(group_in.at[chunk, 1:outer], recv_group.at[chunk])
        blocks = [group[chunk, far]] + [group_in[chunk, step] for step in range(1, outer)]
        logs = [piece[own_rows:] for piece in blocks]
        top = functools.reduce(jnp.maximum, logs)
        summed, total = 0.0, 0.0
        for step in range(outer):
            weight = jnp.exp2(logs[step] - top)
            summed = summed + weight * blocks[step][:own_rows]
            total = total + weight
        own[chunk, far] = summed / total

        def send(step, carry):
            pltpu.make_async_remote_copy(
                src_ref=own.at[chunk, far], dst_ref=own.at[chunk, far],
                send_sem=send_own.at[chunk], recv_sem=recv_own.at[chunk],
                device_id=far_device(step), device_id_type=MESH,
            ).start()
            return carry

        lax.fori_loop(1, outer, send, 0)

    def spread(chunk):
        wait_for(own.at[chunk, 1:outer], recv_own.at[chunk])
        gathered[chunk, near] = own[chunk].reshape(slice_rows, 128).astype(BF16)

        def send(step, carry):
            pltpu.make_async_remote_copy(
                src_ref=gathered.at[chunk, near], dst_ref=gathered.at[chunk, near],
                send_sem=send_read.at[chunk], recv_sem=recv_read.at[chunk],
                device_id=near_device(step), device_id_type=MESH,
            ).start()
            return carry

        lax.fori_loop(1, inner, send, 0)

    def turn(step, carry):
        attend(step, 0, pairs)
        send_first(step)

        @pl.when(step >= 2)
        def _():
            merge_second(step - 2)

        @pl.when(step >= 1)
        def _():
            merge_first(step - 1)

        return carry

    lax.fori_loop(0, chunks - 1, turn, 0)
    attend(chunks - 1, 0, pairs - 1)
    spread(chunks - 4)
    merge_second(chunks - 3)
    attend(chunks - 1, pairs - 1, pairs)
    send_first(chunks - 1)
    merge_first(chunks - 2)

    def latent_side(chunk):
        wait_for(gathered.at[chunk, 1:inner], recv_read.at[chunk])
        every = gathered[chunk].reshape(pairs, block, 128)
        read1 = jnp.concatenate([every[pair] for pair in range(pairs)], axis=1)
        rows = slice(chunk * block, chunk * block + block)
        state = (latents[rows, :].astype(F32) + dot(read1, w_o1[...])).astype(BF16)
        return dot(state, w_k2[...]).astype(BF16), dot(state, w_v2[...]).astype(BF16)

    high = cell_count // 4

    def leave(step):
        planes = pl.ds(step * (size_x // 4), size_x // 4)
        return pltpu.make_async_copy(pad.at[planes, 0:size_y], out.at[planes], store_sem.at[step])

    def absorb(part_index, keys, values, between):
        last = part_index == 1
        span = keys.shape[0]
        per = size_x // 4

        def rows_of(step, carry):
            rows = pl.ds(pl.multiple_of(step * high, high), high)

            def scores(pair, half):
                return dot_t(jnp.where(lane // 64 == half, q2[rows, columns(pair)], BF16(0)), keys[:, columns(pair)])

            def update(score, pair, half):
                top = jnp.max(score, axis=1, keepdims=True)
                shrink = None
                if last:
                    before = tops[2 * pair + half, rows, :]
                    top = jnp.maximum(before, top)
                    shrink = jnp.exp2((before - top) * scale)
                    top = jnp.concatenate([top] * (span // 128), axis=1)
                else:
                    tops[2 * pair + half, rows, :] = jnp.broadcast_to(top, (high, 128))
                return jnp.exp2((score - top) * scale).astype(BF16), shrink

            def add(weight, shrink, pair, half):
                both = jnp.where(lane // 64 == half, values[:, columns(pair)], BF16(1))
                summed = dot(weight, both)
                if not last:
                    sums[2 * pair + half, rows, :] = summed
                    return None
                summed = summed + shrink * sums[2 * pair + half, rows, :]
                return summed / pltpu.roll(summed, 64, 1)

            items = [(pair, half) for pair in range(pairs) for half in range(2)]
            score, weight, shrink, found, joined = scores(*items[0]), None, None, {}, []
            for j in range(len(items) + 1):
                later = scores(*items[j + 1]) if j + 1 < len(items) else None
                new = update(score, *items[j]) if j < len(items) else (None, None)
                if j > 0:
                    found[items[j - 1]] = add(weight, shrink, *items[j - 1])
                    if last and items[j - 1][1] == 1:
                        pair = items[j - 1][0]
                        joined.append(jnp.where(lane < 64, found[(pair, 0)], found[(pair, 1)]).astype(BF16))
                score, (weight, shrink) = later, new
            if last:
                residual = masked[pl.ds(step * per, per)].reshape(high, width).astype(F32)
                result = residual + dot(jnp.concatenate(joined, axis=1), w_o2[...])
                pad[pl.ds(step * per, per), 0:size_y] = result.reshape(per, size_y, size_z, width)
                leave(step).start()
            else:
                between(step)
            return carry

        lax.fori_loop(0, 4, rows_of, 0)

    lax.fori_loop(0, 4, project_second, 0)
    spread(chunks - 3)
    merge_second(chunks - 2)
    merge_first(chunks - 1)
    early = [latent_side(0), latent_side(1)]

    def between(step):
        @pl.when(step == 0)
        def _():
            spread(chunks - 2)
            merge_second(chunks - 1)

        @pl.when(step == 2)
        def _():
            spread(chunks - 1)

    absorb(
        0,
        jnp.concatenate([keys for keys, _ in early], axis=0),
        jnp.concatenate([values for _, values in early], axis=0),
        between,
    )
    late = [latent_side(2), latent_side(3)]
    absorb(
        1,
        jnp.concatenate([keys for keys, _ in late], axis=0),
        jnp.concatenate([values for _, values in late], axis=0),
        None,
    )
    for chunk in range(chunks):
        wait_for(part_in.at[chunk, 1:inner], send_part.at[chunk])
        wait_for(stat_in.at[chunk, 1:inner], send_stat.at[chunk])
        wait_for(group_in.at[chunk, 1:outer], send_group.at[chunk])
        wait_for(own.at[chunk, 1:outer], send_own.at[chunk])
        wait_for(gathered.at[chunk, 1:inner], send_read.at[chunk])
    for step in range(4):
        leave(step).wait()


def layer_call(scale, cells, mask, conv, latents, *weights):
    chunks = 4
    size_x, size_y, size_z, width = cells.shape
    count = size_x * size_y * size_z
    rows = latents.shape[0] // chunks * (width // 128)
    inner = 8
    outer = lax.axis_size("wide") // inner * lax.axis_size("narrow")
    slice_rows = rows // inner
    own_rows = slice_rows // outer
    return pl.pallas_call(
        functools.partial(layer_kernel, scale, chunks),
        out_shape=jax.ShapeDtypeStruct(cells.shape, F32),
        in_specs=[vmem()] * 3 + [pl.BlockSpec(memory_space=pl.ANY)] * 9,
        out_specs=pl.BlockSpec(memory_space=pl.ANY),
        scratch_shapes=[pltpu.VMEM(array.shape, array.dtype) for array in (latents, *weights)]
        + [
            pltpu.VMEM(cells.shape, BF16),
            pltpu.VMEM((2, size_y, size_z, width), BF16),
            pltpu.VMEM((2, size_x, size_z, width), BF16),
            pltpu.VMEM((2, 2, size_z, width), BF16),
            pltpu.VMEM((size_x + 2, size_y + 2, size_z, width), F32),
            pltpu.VMEM((27, 8, width), F32),
            pltpu.VMEM((count, width), BF16),
            pltpu.VMEM(latents.shape, BF16),
            pltpu.VMEM((count, width), BF16),
            pltpu.VMEM((count, width), BF16),
            pltpu.VMEM((count, width), BF16),
            pltpu.VMEM((chunks, rows, 128), BF16),
            pltpu.VMEM((chunks, inner, 8, 128), F32),
            pltpu.VMEM((chunks, inner, slice_rows, 128), BF16),
            pltpu.VMEM((chunks, inner, 8, 128), F32),
            pltpu.VMEM((chunks, outer, 2 * own_rows, 128), F32),
            pltpu.VMEM((chunks, outer, 2 * own_rows, 128), F32),
            pltpu.VMEM((chunks, outer, own_rows, 128), F32),
            pltpu.VMEM((chunks, inner, slice_rows, 128), BF16),
            pltpu.VMEM((width // 64, count, 128), F32),
            pltpu.VMEM((width // 64, count, 128), F32),
        ]
        + [pltpu.SemaphoreType.DMA((8,))] * 2
        + [pltpu.SemaphoreType.DMA((chunks,))] * 10
        + [pltpu.SemaphoreType.DMA((9,)), pltpu.SemaphoreType.DMA((4,))],
        compiler_params=pltpu.CompilerParams(
            collective_id=0, has_side_effects=True, vmem_limit_bytes=62 * 2**20
        ),
        name="layer",
    )(cells, mask, conv, latents, *weights)


def per_device(
    flow_field, fluid_mask, conv_weight, latents,
    w_query1, w_key1, w_value1, w_out1, w_query2, w_key2, w_value2, w_out2,
):
    size_x, size_y, size_z, width = flow_field.shape
    scale = 1.8 / math.sqrt(width // HEADS) * math.log2(math.e)
    result = layer_call(
        scale, flow_field, fluid_mask, conv_weight, latents,
        w_query1, w_key1, w_value1, w_query2, w_out1, w_key2, w_value2, w_out2,
    )
    return result.reshape(size_x, size_y, size_z, width)


def solution(mesh):
    cells = P("wide", "narrow", None, None)
    return jax.shard_map(
        per_device,
        mesh=mesh,
        in_specs=(cells, P("wide", "narrow", None)) + (P(),) * 10,
        out_specs=cells,
        check_vma=False,
    )
```
